256 devices in a mesh: dp: 16 (over z_hi, x, core), uly: 16 (over z_lo, y).
Axes of the slice: x: 4, y: 4, z: 8 (z_hi: 2, z_lo: 4; z = z_hi * 4 + z_lo), core: 2. Of those that a mesh axis runs over, the one named last changes fastest.
Arguments:
- queries: bfloat16 [16, 2048, 4096], P('dp', 'uly'), may hold values from -6 to 6
- key_rows: bfloat16 [16, 2048, 4096], P('dp', 'uly'), may hold values from -5 to 5
- value_rows: bfloat16 [16, 2048, 4096], P('dp', 'uly'), may hold values from -5 to 5
- out_grad: bfloat16 [16, 2048, 4096], P('dp', 'uly'), may hold values from -5 to 5
- prev_grads: bfloat16 [16, 5120, 4096], P('dp', None, 'uly'), may hold values from -1.5 to 1.5
Outputs:
- attended: bfloat16 [16, 2048, 4096], P('dp', 'uly')
- query_grad: bfloat16 [16, 2048, 4096], P('dp', 'uly')
- key_grad: bfloat16 [16, 2048, 4096], P('dp', 'uly')
- value_grad: bfloat16 [16, 2048, 4096], P('dp', 'uly')
- grad_sum: float32 [5120, 4096], P('dp', 'uly')
The draws below stay inside these ranges and needn't reach their ends.
All inputs are finite; a program needn't handle non-finite values.
Results may differ from the reference program's by a relative error of at most 0.012.
Values may be sent and summed in bfloat16 or wider, within the bound.
No kernel may reach another device: no remote copies, remote signals or barrier semaphores. Data moves between devices by JAX's collectives and lax.ppermute only.
A program may use at most 128 MiB of HBM per device.

```python
import math
import jax
import jax.numpy as jnp
from jax import lax

D = 5120
HD = 128
HEADS = 32
SEQ = 2048
GCOLS = 4096
N_DP = 16


def drawn_pair(key):
    base_key = jax.random.fold_in(key, 7)
    query_key, key_key = jax.random.split(base_key, 2)
    width = HEADS * HD
    query_draw = jnp.clip(jax.random.normal(query_key, (N_DP, SEQ, width), jnp.float32), -5.0, 5.0)
    key_draw = jnp.clip(jax.random.normal(key_key, (N_DP, SEQ, width), jnp.float32), -5.0, 5.0)
    return (query_draw, key_draw)


def draw_queries(key, part):
    return drawn_pair(key)[0].astype(jnp.bfloat16)


def draw_key_rows(key, part):
    return drawn_pair(key)[1].astype(jnp.bfloat16)


def with_spikes(result, own_key, source, target, blocks, factor):
    def block_of(axis_at):
        return (jnp.arange(result.shape[axis_at]) // (result.shape[axis_at] // blocks)).reshape((-1,) + (1,) * (result.ndim - 1 - axis_at))

    one_side = jax.random.permutation(own_key, blocks)[block_of(target)]
    second = (block_of(target) + blocks // 2) % blocks
    return jnp.where((block_of(source) == one_side) | (block_of(source) == second), factor * result, result)


def shard_levels(key, dims, pieces, smallest, top_value):
    level = 1.0
    for dim, shards_of in pieces:
        draws = jax.random.uniform(jax.random.fold_in(jax.random.fold_in(key, 6), dim), (shards_of,), jnp.float32, smallest / len(pieces), top_value / len(pieces))
        level = level * jnp.repeat(jnp.exp(draws), dims[dim] // shards_of).reshape((-1,) + (1,) * (len(dims) - 1 - dim))
    return level


def bell_draw(key, dims, scale, bound, cuts=(), held_as=jnp.bfloat16):
    entries = scale * jax.random.normal(key, dims, jnp.float32)
    if cuts:
        entries = entries * shard_levels(key, dims, cuts, -0.22, 0.18)
    return jnp.clip(entries, -bound, bound).astype(held_as)


def gaussian_with(own_key, shape, deviation, most, cuts, heavy, held_as=jnp.bfloat16):
    entries = deviation * jax.random.normal(own_key, shape, jnp.float32)
    if cuts:
        entries = entries * shard_levels(own_key, shape, cuts, -0.22, 0.18)
    return jnp.clip(with_spikes(entries, jax.random.fold_in(own_key, 3), *heavy), -most, most).astype(held_as)


def setup_inputs(seed: int = 0) -> dict:
    keys = jax.random.split(jax.random.key(seed), 6)
    return {
        "queries": draw_queries(jax.random.fold_in(keys[5], 71), 0),
        "key_rows": draw_key_rows(jax.random.fold_in(keys[5], 71), 0),
        "value_rows": bell_draw(keys[2], (N_DP, SEQ, HEADS * HD), 1.0, 5.0, ((0, 16), (1, 16))),
        "out_grad": bell_draw(keys[3], (N_DP, SEQ, HEADS * HD), 1.0, 5.0, ((0, 16), (1, 16))),
        "prev_grads": gaussian_with(keys[4], (N_DP, D, GCOLS), 0.25, 1.5, ((0, 16), (2, 16)), (0, 1, 16, 2.0)),
    }


def attend_one(items):
    query_head, key_head, value_head, grad_head = items
    score_scale = 1.0 / math.sqrt(HD)
    scores = jnp.dot(query_head, key_head.T, preferred_element_type=jnp.float32) * score_scale
    row_max = lax.optimization_barrier(jnp.max(scores, axis=-1, keepdims=True))
    shifted = jnp.exp(scores - row_max)
    prob_rows = shifted / lax.optimization_barrier(jnp.sum(shifted, axis=-1, keepdims=True))
    prob_low = prob_rows.astype(jnp.bfloat16)
    attended = jnp.dot(prob_low, value_head, preferred_element_type=jnp.float32).astype(jnp.bfloat16)
    dprobs = jnp.dot(grad_head, value_head.T, preferred_element_type=jnp.float32)
    row_delta = lax.optimization_barrier(jnp.sum(prob_rows * dprobs, axis=-1, keepdims=True))
    dscores = (prob_rows * (dprobs - row_delta) * score_scale).astype(jnp.bfloat16)
    query_grad = jnp.dot(dscores, key_head, preferred_element_type=jnp.float32).astype(jnp.bfloat16)
    key_grad = jnp.dot(dscores.T, query_head, preferred_element_type=jnp.float32).astype(jnp.bfloat16)
    value_grad = jnp.dot(prob_low.T, grad_head, preferred_element_type=jnp.float32).astype(jnp.bfloat16)
    return (attended, query_grad, key_grad, value_grad)

def split_heads(array):
    return array.reshape(SEQ, HEADS, HD).transpose(1, 0, 2)

def join_heads(array):
    return array.transpose(1, 0, 2).reshape(SEQ, HEADS * HD)

def attend_clip(items):
    heads_in = (split_heads(items[0]), split_heads(items[1]), split_heads(items[2]), split_heads(items[3]))
    results = lax.map(attend_one, heads_in)
    return (join_heads(results[0]), join_heads(results[1]), join_heads(results[2]), join_heads(results[3]))

def reference(queries, key_rows, value_rows, out_grad, prev_grads):
    attended, query_grad, key_grad, value_grad = lax.map(attend_clip, (queries, key_rows, value_rows, out_grad))
    grad_sum = lax.optimization_barrier(jnp.sum(prev_grads.astype(jnp.float32), axis=0))
    return (attended, query_grad, key_grad, value_grad, grad_sum)
```

```python
import functools
import math

import jax
import jax.numpy as jnp
from jax import lax
from jax.experimental import pallas as pl
from jax.experimental.pallas import tpu as pltpu
from jax.sharding import PartitionSpec as P

HD = 128
SCORE_SCALE = 1.0 / math.sqrt(HD)
LOG2_E = math.log2(math.e)


def dot(left, right, left_dim, right_dim):
    return lax.dot_general(
        left,
        right,
        (((left_dim,), (right_dim,)), ((), ())),
        preferred_element_type=jnp.float32,
    )


def attend_body(block_chunks, in_ref, out_ref, kgrad_acc, vgrad_acc):
    step = pl.program_id(0)
    chunks, _, tok_rows, _ = in_ref.shape
    seq_len = chunks * tok_rows
    block_rows = block_chunks * tok_rows

    @pl.when(step == 0)
    def _():
        kgrad_acc[...] = jnp.zeros_like(kgrad_acc)
        vgrad_acc[...] = jnp.zeros_like(vgrad_acc)

    rows = pl.ds(step * block_chunks, block_chunks)
    query = in_ref[rows, 0].reshape(block_rows, HD)
    grad = in_ref[rows, 3].reshape(block_rows, HD)
    key = in_ref[:, 1].reshape(seq_len, HD)
    value = in_ref[:, 2].reshape(seq_len, HD)

    scores = dot(query, key, 1, 1)
    row_max = jnp.max(scores, axis=1, keepdims=True)
    shifted = jnp.exp2((scores - row_max) * (SCORE_SCALE * LOG2_E))
    inverse = 1.0 / jnp.sum(shifted, axis=1, keepdims=True)
    shifted_low = shifted.astype(jnp.bfloat16)
    attended = dot(shifted_low, value, 1, 0) * inverse
    grad_wide = grad.astype(jnp.float32)
    row_delta = jnp.sum(grad_wide * attended, axis=1, keepdims=True)
    dprobs = dot(grad, value, 1, 1)
    dscores = (shifted * (dprobs - row_delta)).astype(jnp.bfloat16)
    inverse_scaled = inverse * SCORE_SCALE
    query_grad = dot(dscores, key, 1, 0) * inverse_scaled
    vgrad_acc[...] += dot((grad_wide * inverse).astype(jnp.bfloat16), shifted_low, 0, 0)
    kgrad_acc[...] += dot(
        (query.astype(jnp.float32) * inverse_scaled).astype(jnp.bfloat16), dscores, 0, 0
    )
    out_ref[rows, 0] = attended.astype(jnp.bfloat16).reshape(block_chunks, tok_rows, HD)
    out_ref[rows, 1] = query_grad.astype(jnp.bfloat16).reshape(block_chunks, tok_rows, HD)

    @pl.when(step == pl.num_programs(0) - 1)
    def _():
        out_ref[:, 2] = kgrad_acc[...].T.astype(jnp.bfloat16).reshape(chunks, tok_rows, HD)
        out_ref[:, 3] = vgrad_acc[...].T.astype(jnp.bfloat16).reshape(chunks, tok_rows, HD)


def attend_head(packed):
    chunks, _, tok_rows, _ = packed.shape
    seq_len = chunks * tok_rows
    block_chunks = max(1, min(chunks, 512 // tok_rows))
    return pl.pallas_call(
        functools.partial(attend_body, block_chunks),
        grid=(chunks // block_chunks,),
        in_specs=[pl.BlockSpec(packed.shape, lambda step: (0, 0, 0, 0))],
        out_specs=pl.BlockSpec(packed.shape, lambda step: (0, 0, 0, 0)),
        out_shape=jax.ShapeDtypeStruct(packed.shape, jnp.bfloat16),
        scratch_shapes=[
            pltpu.VMEM((HD, seq_len), jnp.float32),
            pltpu.VMEM((HD, seq_len), jnp.float32),
        ],
        compiler_params=pltpu.CompilerParams(vmem_limit_bytes=60 * 1024 * 1024),
        cost_estimate=pl.CostEstimate(
            flops=12 * seq_len * seq_len * HD,
            bytes_accessed=4 * packed.size,
            transcendentals=seq_len * seq_len,
        ),
        name="attend_head",
    )(packed)


def pack_body(*refs):
    *in_refs, out_ref = refs
    for j, in_ref in enumerate(in_refs):
        for target in range(out_ref.shape[0]):
            out_ref[target, j] = in_ref[0, :, target * HD : (target + 1) * HD]


def pack_heads(arrays, first, count, step_heads):
    tok_rows = arrays[0].shape[1]
    offset = first // step_heads
    return pl.pallas_call(
        pack_body,
        grid=(count // step_heads,),
        in_specs=[
            pl.BlockSpec((1, tok_rows, step_heads * HD), lambda step: (0, 0, offset + step))
        ]
        * len(arrays),
        out_specs=pl.BlockSpec(
            (step_heads, len(arrays), tok_rows, HD), lambda step: (step, 0, 0, 0)
        ),
        out_shape=jax.ShapeDtypeStruct((count, len(arrays), tok_rows, HD), jnp.bfloat16),
        compiler_params=pltpu.CompilerParams(vmem_limit_bytes=60 * 1024 * 1024),
        name="pack_heads",
    )(*arrays)


def unpack_body(count, in_ref, *refs):
    for j, out_ref in enumerate(refs[-count:]):
        for source in range(in_ref.shape[0]):
            out_ref[0, :, source * HD : (source + 1) * HD] = in_ref[source, j]


def unpack_heads(returned, previous, first, width, step_heads):
    heads, count, tok_rows, _ = returned.shape
    offset = first // step_heads
    return pl.pallas_call(
        functools.partial(unpack_body, count),
        grid=(heads // step_heads,),
        in_specs=[
            pl.BlockSpec((step_heads, count, tok_rows, HD), lambda step: (step, 0, 0, 0))
        ]
        + [pl.BlockSpec(memory_space=pl.ANY)] * len(previous),
        out_specs=[
            pl.BlockSpec((1, tok_rows, step_heads * HD), lambda step: (0, 0, offset + step))
        ]
        * count,
        out_shape=[jax.ShapeDtypeStruct((1, tok_rows, width), jnp.bfloat16)] * count,
        input_output_aliases={1 + j: j for j in range(len(previous))},
        compiler_params=pltpu.CompilerParams(vmem_limit_bytes=16 * 1024 * 1024),
        name="unpack_heads",
    )(returned, *previous)


def on_device(queries, key_rows, value_rows, out_grad, prev_grads):
    arrays = (queries, key_rows, value_rows, out_grad)
    width = queries.shape[2]
    uly_count = lax.axis_size("uly")
    own_heads = width // uly_count // HD
    step_heads = math.gcd(4, uly_count)
    grad_sum = lax.psum_scatter(prev_grads[0], "dp", scatter_dimension=0, tiled=True)
    outputs = ()
    results = []
    for turn in range(own_heads):
        packed = pack_heads(arrays, turn * uly_count, uly_count, step_heads)
        arrived = lax.all_to_all(packed, "uly", split_axis=0, concat_axis=0, tiled=True)
        results.append(attend_head(arrived))
    results[-1], grad_sum = lax.optimization_barrier((results[-1], grad_sum))
    for turn in range(own_heads):
        returned = lax.all_to_all(results[turn], "uly", split_axis=0, concat_axis=0, tiled=True)
        outputs = unpack_heads(returned, outputs, turn * uly_count, width, step_heads)
    return (*outputs, grad_sum.astype(jnp.float32))


def solution(mesh):
    return jax.shard_map(
        on_device,
        mesh=mesh,
        in_specs=(
            P("dp", "uly", None),
            P("dp", "uly", None),
            P("dp", "uly", None),
            P("dp", "uly", None),
            P("dp", None, "uly"),
        ),
        out_specs=(
            P("dp", "uly", None),
            P("dp", "uly", None),
            P("dp", "uly", None),
            P("dp", "uly", None),
            P("dp", "uly"),
        ),
        check_vma=False,
    )
```

```python
import functools
import math

import jax
import jax.numpy as jnp
from jax import lax
from jax.experimental import pallas as pl
from jax.experimental.pallas import tpu as pltpu
from jax.sharding import PartitionSpec as P

HD = 128
SCORE_SCALE = 1.0 / math.sqrt(HD)
LOG2_E = math.log2(math.e)


def dot(left, right, left_dim, right_dim):
    return lax.dot_general(
        left,
        right,
        (((left_dim,), (right_dim,)), ((), ())),
        preferred_element_type=jnp.float32,
    )


def attend_body(block_chunks, in_ref, out_ref, kgrad_acc, vgrad_acc):
    step = pl.program_id(0)
    chunks, _, tok_rows, _ = in_ref.shape
    seq_len = chunks * tok_rows
    block_rows = block_chunks * tok_rows

    @pl.when(step == 0)
    def _():
        kgrad_acc[...] = jnp.zeros_like(kgrad_acc)
        vgrad_acc[...] = jnp.zeros_like(vgrad_acc)

    rows = pl.ds(step * block_chunks, block_chunks)
    query = in_ref[rows, 0].reshape(block_rows, HD)
    grad = in_ref[rows, 3].reshape(block_rows, HD)
    key = in_ref[:, 1].reshape(seq_len, HD)
    value = in_ref[:, 2].reshape(seq_len, HD)

    scores = dot(query, key, 1, 1)
    row_max = jnp.max(scores, axis=1, keepdims=True)
    shifted = jnp.exp2((scores - row_max) * (SCORE_SCALE * LOG2_E))
    inverse = 1.0 / jnp.sum(shifted, axis=1, keepdims=True)
    shifted_low = shifted.astype(jnp.bfloat16)
    attended = dot(shifted_low, value, 1, 0) * inverse
    grad_wide = grad.astype(jnp.float32)
    row_delta = jnp.sum(grad_wide * attended, axis=1, keepdims=True)
    dprobs = dot(grad, value, 1, 1)
    dscores = (shifted * (dprobs - row_delta)).astype(jnp.bfloat16)
    inverse_scaled = inverse * SCORE_SCALE
    query_grad = dot(dscores, key, 1, 0) * inverse_scaled
    vgrad_acc[...] += dot((grad_wide * inverse).astype(jnp.bfloat16), shifted_low, 0, 0)
    kgrad_acc[...] += dot(
        (query.astype(jnp.float32) * inverse_scaled).astype(jnp.bfloat16), dscores, 0, 0
    )
    out_ref[rows, 0] = attended.astype(jnp.bfloat16).reshape(block_chunks, tok_rows, HD)
    out_ref[rows, 1] = query_grad.astype(jnp.bfloat16).reshape(block_chunks, tok_rows, HD)

    @pl.when(step == pl.num_programs(0) - 1)
    def _():
        out_ref[:, 2] = kgrad_acc[...].T.astype(jnp.bfloat16).reshape(chunks, tok_rows, HD)
        out_ref[:, 3] = vgrad_acc[...].T.astype(jnp.bfloat16).reshape(chunks, tok_rows, HD)


def attend_head(packed):
    chunks, _, tok_rows, _ = packed.shape
    seq_len = chunks * tok_rows
    block_chunks = max(1, min(chunks, 512 // tok_rows))
    return pl.pallas_call(
        functools.partial(attend_body, block_chunks),
        grid=(chunks // block_chunks,),
        in_specs=[pl.BlockSpec(packed.shape, lambda step: (0, 0, 0, 0))],
        out_specs=pl.BlockSpec(packed.shape, lambda step: (0, 0, 0, 0)),
        out_shape=jax.ShapeDtypeStruct(packed.shape, jnp.bfloat16),
        scratch_shapes=[
            pltpu.VMEM((HD, seq_len), jnp.float32),
            pltpu.VMEM((HD, seq_len), jnp.float32),
        ],
        compiler_params=pltpu.CompilerParams(vmem_limit_bytes=60 * 1024 * 1024),
        cost_estimate=pl.CostEstimate(
            flops=12 * seq_len * seq_len * HD,
            bytes_accessed=4 * packed.size,
            transcendentals=seq_len * seq_len,
        ),
        name="attend_head",
    )(packed)


def pack_body(*refs):
    *in_refs, out_ref = refs
    for j, in_ref in enumerate(in_refs):
        for target in range(out_ref.shape[0]):
            out_ref[target, j] = in_ref[0, :, target * HD : (target + 1) * HD]


def pack_heads(arrays, first, count, step_heads):
    tok_rows = arrays[0].shape[1]
    offset = first // step_heads
    return pl.pallas_call(
        pack_body,
        grid=(count // step_heads,),
        in_specs=[
            pl.BlockSpec((1, tok_rows, step_heads * HD), lambda step: (0, 0, offset + step))
        ]
        * len(arrays),
        out_specs=pl.BlockSpec(
            (step_heads, len(arrays), tok_rows, HD), lambda step: (step, 0, 0, 0)
        ),
        out_shape=jax.ShapeDtypeStruct((count, len(arrays), tok_rows, HD), jnp.bfloat16),
        compiler_params=pltpu.CompilerParams(vmem_limit_bytes=60 * 1024 * 1024),
        name="pack_heads",
    )(*arrays)


def unpack_body(count, in_ref, *refs):
    for j, out_ref in enumerate(refs[-count:]):
        for source in range(in_ref.shape[0]):
            out_ref[0, :, source * HD : (source + 1) * HD] = in_ref[source, j]


def unpack_heads(returned, previous, first, width, step_heads):
    heads, count, tok_rows, _ = returned.shape
    offset = first // step_heads
    return pl.pallas_call(
        functools.partial(unpack_body, count),
        grid=(heads // step_heads,),
        in_specs=[
            pl.BlockSpec((step_heads, count, tok_rows, HD), lambda step: (step, 0, 0, 0))
        ]
        + [pl.BlockSpec(memory_space=pl.ANY)] * len(previous),
        out_specs=[
            pl.BlockSpec((1, tok_rows, step_heads * HD), lambda step: (0, 0, offset + step))
        ]
        * count,
        out_shape=[jax.ShapeDtypeStruct((1, tok_rows, width), jnp.bfloat16)] * count,
        input_output_aliases={1 + j: j for j in range(len(previous))},
        compiler_params=pltpu.CompilerParams(vmem_limit_bytes=60 * 1024 * 1024),
        name="unpack_heads",
    )(returned, *previous)


def half_terms(terms):
    count = lax.axis_size("dp")
    half = count // 2
    place = lax.axis_index("dp") % half
    rows = terms.shape[0] // half
    parts = []
    for s in range(half):
        part = lax.dynamic_slice_in_dim(terms, (place ^ s) * rows, rows, 0)
        if s:
            part = lax.ppermute(part, "dp", [(a, a ^ s) for a in range(count)])
        parts.append(part)
    return parts


def half_sums(parts):
    total = sum(part.astype(jnp.float32) for part in parts)
    return total.astype(parts[0].dtype).reshape(2, parts[0].shape[0] // 2, -1)


def both_halves(sums):
    half = lax.axis_size("dp") // 2
    side = lax.axis_index("dp") // half
    arrived = []
    for flip in range(2):
        block = lax.dynamic_index_in_dim(sums, side ^ flip, 0, keepdims=False)
        pairs = [(h * half + a, 2 * a + (h ^ flip)) for h in range(2) for a in range(half)]
        arrived.append(lax.ppermute(block, "dp", pairs))
    return arrived


def on_device(queries, key_rows, value_rows, out_grad, prev_grads):
    arrays = (queries, key_rows, value_rows, out_grad)
    width = queries.shape[2]
    uly_count = lax.axis_size("uly")
    own_heads = width // uly_count // HD
    step_heads = math.gcd(8, uly_count)
    outputs = ()
    results = []
    for turn in range(own_heads):
        packed = pack_heads(arrays, turn * uly_count, uly_count, step_heads)
        if turn == 0:
            packed, terms = lax.optimization_barrier((packed, prev_grads[0]))
            parts = half_terms(terms)
        else:
            packed, *parts[1:3] = lax.optimization_barrier((packed, *parts[1:3]))
        arrived = lax.all_to_all(packed, "uly", split_axis=0, concat_axis=0, tiled=True)
        results.append(attend_head(arrived))
    results[0], parts = lax.optimization_barrier((results[0], parts))
    results[0], sums = lax.optimization_barrier((results[0], half_sums(parts)))
    results[-1], arrived = lax.optimization_barrier((results[-1], both_halves(sums)))
    grad_sum = arrived[0].astype(jnp.float32) + arrived[1].astype(jnp.float32)
    for turn in range(own_heads):
        returned = lax.all_to_all(results[turn], "uly", split_axis=0, concat_axis=0, tiled=True)
        outputs = unpack_heads(returned, outputs, turn * uly_count, width, step_heads)
    return (*outputs, grad_sum)


def solution(mesh):
    return jax.shard_map(
        on_device,
        mesh=mesh,
        in_specs=(
            P("dp", "uly", None),
            P("dp", "uly", None),
            P("dp", "uly", None),
            P("dp", "uly", None),
            P("dp", None, "uly"),
        ),
        out_specs=(
            P("dp", "uly", None),
            P("dp", "uly", None),
            P("dp", "uly", None),
            P("dp", "uly", None),
            P("dp", "uly"),
        ),
        check_vma=False,
    )
```

```python
import functools
import math

import jax
import jax.numpy as jnp
from jax import lax
from jax.experimental import pallas as pl
from jax.experimental.pallas import tpu as pltpu
from jax.sharding import PartitionSpec as P

HD = 128
SCORE_SCALE = 1.0 / math.sqrt(HD)
LOG2_E = math.log2(math.e)


def dot(left, right, left_dim, right_dim):
    return lax.dot_general(
        left,
        right,
        (((left_dim,), (right_dim,)), ((), ())),
        preferred_element_type=jnp.float32,
    )


def attend_body(block_chunks, in_ref, out_ref, kgrad_acc, vgrad_acc):
    step = pl.program_id(0)
    chunks, _, tok_rows, _ = in_ref.shape
    seq_len = chunks * tok_rows
    block_rows = block_chunks * tok_rows

    @pl.when(step == 0)
    def _():
        kgrad_acc[...] = jnp.zeros_like(kgrad_acc)
        vgrad_acc[...] = jnp.zeros_like(vgrad_acc)

    rows = pl.ds(step * block_chunks, block_chunks)
    query = in_ref[rows, 0].reshape(block_rows, HD)
    grad = in_ref[rows, 3].reshape(block_rows, HD)
    key = in_ref[:, 1].reshape(seq_len, HD)
    value = in_ref[:, 2].reshape(seq_len, HD)

    scores = dot(query, key, 1, 1)
    row_max = jnp.max(scores, axis=1, keepdims=True)
    shifted = jnp.exp2((scores - row_max) * (SCORE_SCALE * LOG2_E))
    inverse = 1.0 / jnp.sum(shifted, axis=1, keepdims=True)
    shifted_low = shifted.astype(jnp.bfloat16)
    attended = dot(shifted_low, value, 1, 0) * inverse
    grad_wide = grad.astype(jnp.float32)
    row_delta = jnp.sum(grad_wide * attended, axis=1, keepdims=True)
    dprobs = dot(grad, value, 1, 1)
    dscores = (shifted * (dprobs - row_delta)).astype(jnp.bfloat16)
    inverse_scaled = inverse * SCORE_SCALE
    query_grad = dot(dscores, key, 1, 0) * inverse_scaled
    vgrad_acc[...] += dot((grad_wide * inverse).astype(jnp.bfloat16), shifted_low, 0, 0)
    kgrad_acc[...] += dot(
        (query.astype(jnp.float32) * inverse_scaled).astype(jnp.bfloat16), dscores, 0, 0
    )
    out_ref[rows, 0] = attended.astype(jnp.bfloat16).reshape(block_chunks, tok_rows, HD)
    out_ref[rows, 1] = query_grad.astype(jnp.bfloat16).reshape(block_chunks, tok_rows, HD)

    @pl.when(step == pl.num_programs(0) - 1)
    def _():
        out_ref[:, 2] = kgrad_acc[...].T.astype(jnp.bfloat16).reshape(chunks, tok_rows, HD)
        out_ref[:, 3] = vgrad_acc[...].T.astype(jnp.bfloat16).reshape(chunks, tok_rows, HD)


def attend_head(packed):
    chunks, _, tok_rows, _ = packed.shape
    seq_len = chunks * tok_rows
    block_chunks = max(1, min(chunks, 512 // tok_rows))
    return pl.pallas_call(
        functools.partial(attend_body, block_chunks),
        grid=(chunks // block_chunks,),
        in_specs=[pl.BlockSpec(packed.shape, lambda step: (0, 0, 0, 0))],
        out_specs=pl.BlockSpec(packed.shape, lambda step: (0, 0, 0, 0)),
        out_shape=jax.ShapeDtypeStruct(packed.shape, jnp.bfloat16),
        scratch_shapes=[
            pltpu.VMEM((HD, seq_len), jnp.float32),
            pltpu.VMEM((HD, seq_len), jnp.float32),
        ],
        compiler_params=pltpu.CompilerParams(vmem_limit_bytes=44 * 1024 * 1024),
        cost_estimate=pl.CostEstimate(
            flops=12 * seq_len * seq_len * HD,
            bytes_accessed=4 * packed.size,
            transcendentals=seq_len * seq_len,
        ),
        name="attend_head",
    )(packed)


def pack_body(*refs):
    *in_refs, out_ref = refs
    for j, in_ref in enumerate(in_refs):
        for target in range(out_ref.shape[0]):
            out_ref[target, j] = in_ref[0, :, target * HD : (target + 1) * HD]


def pack_heads(arrays, first, count, step_heads):
    tok_rows = arrays[0].shape[1]
    offset = first // step_heads
    return pl.pallas_call(
        pack_body,
        grid=(count // step_heads,),
        in_specs=[
            pl.BlockSpec((1, tok_rows, step_heads * HD), lambda step: (0, 0, offset + step))
        ]
        * len(arrays),
        out_specs=pl.BlockSpec(
            (step_heads, len(arrays), tok_rows, HD), lambda step: (step, 0, 0, 0)
        ),
        out_shape=jax.ShapeDtypeStruct((count, len(arrays), tok_rows, HD), jnp.bfloat16),
        compiler_params=pltpu.CompilerParams(vmem_limit_bytes=60 * 1024 * 1024),
        name="pack_heads",
    )(*arrays)


def unpack_body(count, in_ref, *refs):
    for j, out_ref in enumerate(refs[-count:]):
        for source in range(in_ref.shape[0]):
            out_ref[0, :, source * HD : (source + 1) * HD] = in_ref[source, j]


def unpack_heads(returned, previous, first, width, step_heads, vmem_mib):
    heads, count, tok_rows, _ = returned.shape
    offset = first // step_heads
    return pl.pallas_call(
        functools.partial(unpack_body, count),
        grid=(heads // step_heads,),
        in_specs=[
            pl.BlockSpec((step_heads, count, tok_rows, HD), lambda step: (step, 0, 0, 0))
        ]
        + [pl.BlockSpec(memory_space=pl.ANY)] * len(previous),
        out_specs=[
            pl.BlockSpec((1, tok_rows, step_heads * HD), lambda step: (0, 0, offset + step))
        ]
        * count,
        out_shape=[jax.ShapeDtypeStruct((1, tok_rows, width), jnp.bfloat16)] * count,
        input_output_aliases={1 + j: j for j in range(len(previous))},
        compiler_params=pltpu.CompilerParams(vmem_limit_bytes=vmem_mib * 1024 * 1024),
        name="unpack_heads",
    )(returned, *previous)


def half_terms(terms):
    count = lax.axis_size("dp")
    half = count // 2
    place = lax.axis_index("dp") % half
    rows = terms.shape[0] // half
    parts = []
    for s in range(half):
        part = lax.dynamic_slice_in_dim(terms, (place ^ s) * rows, rows, 0)
        if s:
            part = lax.ppermute(part, "dp", [(a, a ^ s) for a in range(count)])
        parts.append(part)
    return parts


def half_sums(parts):
    total = sum(part.astype(jnp.float32) for part in parts)
    return total.astype(parts[0].dtype).reshape(2, parts[0].shape[0] // 2, -1)


def both_halves(sums):
    half = lax.axis_size("dp") // 2
    side = lax.axis_index("dp") // half
    arrived = []
    for flip in range(2):
        block = lax.dynamic_index_in_dim(sums, side ^ flip, 0, keepdims=False)
        pairs = [(h * half + a, 2 * a + (h ^ flip)) for h in range(2) for a in range(half)]
        arrived.append(lax.ppermute(block, "dp", pairs))
    return arrived


def on_device(queries, key_rows, value_rows, out_grad, prev_grads):
    arrays = (queries, key_rows, value_rows, out_grad)
    width = queries.shape[2]
    uly_count = lax.axis_size("uly")
    own_heads = width // uly_count // HD
    step_heads = math.gcd(8, uly_count)
    outputs = ()
    results = []
    for turn in range(own_heads):
        packed = pack_heads(arrays, turn * uly_count, uly_count, step_heads)
        if turn == 0:
            packed, terms = lax.optimization_barrier((packed, prev_grads[0]))
            parts = half_terms(terms)
        else:
            packed, *parts[1:3] = lax.optimization_barrier((packed, *parts[1:3]))
        arrived = lax.all_to_all(packed, "uly", split_axis=0, concat_axis=0, tiled=True)
        results.append(attend_head(arrived))
    results[0], parts = lax.optimization_barrier((results[0], parts))
    results[0], sums = lax.optimization_barrier((results[0], half_sums(parts)))
    results[-1], arrived = lax.optimization_barrier((results[-1], both_halves(sums)))
    grad_sum = arrived[0].astype(jnp.float32) + arrived[1].astype(jnp.float32)
    for turn in range(own_heads):
        returned = lax.all_to_all(results[turn], "uly", split_axis=0, concat_axis=0, tiled=True)
        vmem_mib = 16 if turn == own_heads - 1 else 60
        outputs = unpack_heads(
            returned, outputs, turn * uly_count, width, step_heads, vmem_mib
        )
    return (*outputs, grad_sum)


def solution(mesh):
    return jax.shard_map(
        on_device,
        mesh=mesh,
        in_specs=(
            P("dp", "uly", None),
            P("dp", "uly", None),
            P("dp", "uly", None),
            P("dp", "uly", None),
            P("dp", None, "uly"),
        ),
        out_specs=(
            P("dp", "uly", None),
            P("dp", "uly", None),
            P("dp", "uly", None),
            P("dp", "uly", None),
            P("dp", "uly"),
        ),
        check_vma=False,
    )
```
